256 devices in a mesh: row: 32 (over x, z_lo, core), rep: 8 (over z_hi, y).
Axes of the slice: x: 4, y: 4, z: 8 (z_hi: 2, z_lo: 4; z = z_hi * 4 + z_lo), core: 2. Of those that a mesh axis runs over, the one named last changes fastest.
Arguments:
- features: bfloat16 [65536, 128], P(('row', 'rep')), may hold values from -6 to 6
- degrees: int32 [65536], P('row'), may hold values from 8 to 127
- tile_cols: int32 [512, 32, 4], P('row', 'rep'), may hold values from 0 to 15
- tile_counts: int32 [512, 32], P('row', 'rep'), may hold values from 1 to 4, as said below
- tiles: bfloat16 [512, 32, 4, 128, 128], P('row', 'rep'), may hold values from 0 to 1
- weight: bfloat16 [128, 256], replicated, may hold values from -0.5 to 0.5
- bias: float32 [256], replicated, may hold values from -3 to 3
- cotangent: bfloat16 [65536, 256], P(('row', 'rep')), may hold values from -6 to 6
Outputs:
- hidden: bfloat16 [65536, 256], P(('row', 'rep'))
- grad_weight: float32 [128, 256], replicated
- grad_bias: float32 [256], replicated
The draws below stay inside these ranges and needn't reach their ends.
Inputs may be any that keep to these rules, and one draw needn't show every extreme that they name: `tile_counts`: every row block has 4 live slots for at least one column slab; slots at or past the count hold values that no output reads.
All inputs are finite; a program needn't handle non-finite values.
Results may differ from the reference program's by a relative error of at most 0.0075.
Values may be sent and summed in bfloat16 or wider, within the bound.
No kernel may reach another device: no remote copies, remote signals or barrier semaphores. Data moves between devices by JAX's collectives and lax.ppermute only.
A program may use at most 64 MiB of HBM per device.

```python
import math
import jax
import jax.numpy as jnp
from jax import lax

F = 128
HID = 256
TILE = 128
RB = 16
KMAX = 4
SLABS = 32
NODES = 65536
BLOCKS = 512


def draw_tile_counts(key, part):
    key = jax.random.fold_in(key, 11)
    first, second, third = jax.random.split(key, 3)
    density = jax.random.randint(first, (BLOCKS, 1), 1, KMAX + 1)
    raw_bits = jax.random.randint(second, (BLOCKS, SLABS), 0, 1048576)
    base_count = 1 + raw_bits % density
    full_section = jax.random.randint(third, (BLOCKS, 1), 0, SLABS)
    section_ids = jnp.arange(SLABS)[None, :]
    return jnp.where(section_ids == full_section, KMAX, base_count).astype(jnp.int32)


def touch_ends(drawn, own_key, smallest, high):
    place = [jax.random.randint(jax.random.fold_in(own_key, axis), (), 0, length) for axis, length in enumerate(drawn.shape)]
    main_axis = drawn.shape.index(max(drawn.shape))
    neighbour = place[:main_axis] + [(place[main_axis] + 1) % drawn.shape[main_axis]] + place[main_axis + 1:]
    return drawn.at[tuple(place)].set(smallest).at[tuple(neighbour)].set(high)


def block_levels(own_key, shape, cuts, low, largest):
    loudness, own = 1.0, jax.random.fold_in(own_key, 6)
    for axis_at, blocks in cuts:
        draws = jnp.exp(jax.random.uniform(jax.random.fold_in(own, axis_at), (blocks,), jnp.float32, low / len(cuts), largest / len(cuts)))
        loudness = loudness * jnp.repeat(draws, shape[axis_at] // blocks).reshape([-1 if axis == axis_at else 1 for axis in range(len(shape))])
    return loudness


def noise(key, shape, deviation, limit, pieces=(), kind=jnp.bfloat16):
    entries = deviation * jax.random.normal(key, shape, jnp.float32)
    if pieces:
        entries = entries * block_levels(key, shape, pieces, -0.22, 0.18)
    return jnp.clip(entries, -limit, limit).astype(kind)


def setup_inputs(seed: int = 0) -> dict:
    key_of = jax.random.split(jax.random.key(seed), 9)
    return {
        "features": noise(key_of[0], (NODES, F), 1.0, 6.0, ((0, 256),)),
        "degrees": touch_ends(jax.random.randint(key_of[1], (NODES,), 8, 128), jax.random.fold_in(key_of[1], 1), 8, 127).astype(jnp.int32),
        "tile_cols": touch_ends(jax.random.randint(key_of[2], (BLOCKS, SLABS, KMAX), 0, RB), jax.random.fold_in(key_of[2], 1), 0, RB - 1).astype(jnp.int32),
        "tile_counts": draw_tile_counts(jax.random.fold_in(key_of[8], 71), 0),
        "tiles": jnp.clip(1.0 * jax.random.uniform(key_of[4], (BLOCKS, SLABS, KMAX, TILE, TILE), jnp.float32) ** block_levels(key_of[4], (BLOCKS, SLABS, KMAX, TILE, TILE), ((0, 32), (1, 8)), -0.2, 0.2), 0.0, 1.0).astype(jnp.bfloat16),
        "weight": noise(key_of[5], (F, HID), F ** -0.5, 0.5),
        "bias": noise(key_of[6], (HID,), 0.5, 3.0, (), jnp.float32),
        "cotangent": noise(key_of[7], (NODES, HID), 1.0, 6.0, ((0, 256),)),
    }


def reference(features, degrees, tile_cols, tile_counts, tiles, weight, bias, cotangent):
    inv_root = lax.rsqrt(degrees.astype(jnp.float32))
    scaled = (features.astype(jnp.float32) * inv_root[:, None]).astype(jnp.bfloat16)
    blocks = scaled.reshape(SLABS, RB, TILE, F)
    slab_index = jnp.arange(SLABS)[:, None]

    def one_block(inputs):
        columns, counts, block_tiles = inputs
        picked = blocks[slab_index, columns].astype(jnp.float32)
        live_slot = jnp.arange(KMAX)[None, :] < counts[:, None]
        picked = jnp.where(live_slot[:, :, None, None], picked, jnp.zeros((), picked.dtype))
        return jnp.einsum('skij,skjf->if', block_tiles.astype(jnp.float32), picked)
    summed = lax.map(one_block, (tile_cols, tile_counts, tiles)).reshape(NODES, F)
    aggregated = (summed * inv_root[:, None]).astype(jnp.bfloat16)
    pre_act = jnp.dot(aggregated, weight, preferred_element_type=jnp.float32) + bias
    hidden = jax.nn.silu(pre_act).astype(jnp.bfloat16)
    gate_sig = jax.nn.sigmoid(pre_act)
    pre_grad = (cotangent.astype(jnp.float32) * gate_sig * (1.0 + pre_act * (1.0 - gate_sig))).astype(jnp.bfloat16)
    grad_scale = 1.0 / math.sqrt(NODES)
    grad_weight = jnp.dot(aggregated.T, pre_grad, preferred_element_type=jnp.float32) * grad_scale
    grad_bias = lax.optimization_barrier(jnp.sum(pre_grad.astype(jnp.float32), axis=0)) * grad_scale
    return (hidden, grad_weight, grad_bias)
```

```python
import functools
import math

import jax
import jax.numpy as jnp
from jax import lax
from jax.experimental import pallas as pl
from jax.experimental.pallas import tpu as pltpu
from jax.sharding import Mesh, PartitionSpec as P

AXES = ("x", "zl", "c", "zh", "y")
SIZES = (4, 4, 2, 2, 4)
ROW = ("x", "zl", "c")
REP = ("zh", "y")
FLAT = ("x", "y")
DEEP = ("zl", "zh", "c")
F = 128
TILE = 128
VMEM = pl.BlockSpec(memory_space=pltpu.VMEM)
SMEM = pl.BlockSpec(memory_space=pltpu.SMEM)
PARAMS = pltpu.CompilerParams(vmem_limit_bytes=40 * 1024 * 1024)


def flat_index(x, zl, c, zh, y):
    return (((x * 4 + zl) * 2 + c) * 2 + zh) * 4 + y


def shard_moves():
    pairs = []
    for x in range(4):
        for zl in range(4):
            for c in range(2):
                for zh in range(2):
                    for y in range(4):
                        group = x * 2 + zl // 2
                        to_x = (x + 2 + group % 4 - y) % 4
                        to_zl = 2 * ((zl // 2) ^ zh ^ (group // 4)) + zl % 2
                        pairs.append(
                            (
                                flat_index(x, zl, c, zh, y),
                                flat_index(to_x, to_zl, c, group // 4, group % 4),
                            )
                        )
    return pairs


def repeat(block, count):
    return jnp.broadcast_to(block[None], (count,) + block.shape)


def exchange(block, axes):
    return lax.all_to_all(block, axes, 0, 0, tiled=True)


def gather_kernel(cols, counts, place, tiles, own, other, out):
    block = pl.program_id(0)
    core, x0, z1 = place[0], place[1], place[2]
    total = jnp.zeros((TILE, F), jnp.float32)
    for side, feats in enumerate((own, other)):
        for z0 in range(2):
            slab = z0 * 2 + (core ^ side)
            live = counts[block * 4 + slab]
            picks = []
            for k in range(4):
                col = cols[(block * 4 + slab) * 4 + k]
                at_x = lax.rem(x0 + 4 - lax.rem(col // 2, 4), 4)
                at_z = (z1 ^ (col // 8)) * 2 + z0
                row = ((at_x * 4 + at_z) * 2 + lax.rem(col, 2)) * TILE
                pick = feats[pl.ds(pl.multiple_of(row, TILE), TILE), :]
                if k > 0:
                    pick = jnp.where(k < live, pick, jnp.zeros_like(pick))
                picks.append(pick)
            for k in (0, 2):
                total += jnp.dot(
                    jnp.concatenate([tiles[0, slab, k], tiles[0, slab, k + 1]], axis=1),
                    jnp.concatenate([picks[k], picks[k + 1]], axis=0),
                    preferred_element_type=jnp.float32,
                )
    out[0] = total


def dense_kernel(parts, inv, weight, bias, cotangent, hidden, grads):
    summed = parts[0]
    for i in range(1, 8):
        summed += parts[i]
    aggregated = (summed * inv[...]).astype(jnp.bfloat16)
    pre_act = jnp.dot(aggregated, weight[...], preferred_element_type=jnp.float32) + bias[...]
    sig = 1.0 / (1.0 + jnp.exp(-pre_act))
    hidden[...] = (pre_act * sig).astype(jnp.bfloat16)
    pre_grad = (
        cotangent[...].astype(jnp.float32) * sig * (1.0 + pre_act * (1.0 - sig))
    ).astype(jnp.bfloat16)
    grad_w = lax.dot_general(
        aggregated, pre_grad, (((0,), (0,)), ((), ())), preferred_element_type=jnp.float32
    )
    grad_b = jnp.sum(pre_grad.astype(jnp.float32), axis=0, keepdims=True)
    grad_b = jnp.broadcast_to(grad_b, (8, 256))
    for i in range(16):
        grads[i, 0:8] = grad_w[i * 8 : i * 8 + 8]
        grads[i, 8:16] = grad_b


def first_sum_kernel(parts, out):
    total = parts[0]
    for i in range(1, 16):
        total += parts[i]
    for i in range(16):
        out[i] = total


def last_sum_kernel(scale, parts, grad_w, grad_b):
    total = parts[0]
    for i in range(1, 16):
        total += parts[i]
    total = total * scale
    for i in range(16):
        grad_w[i] = total[0:8]
    grad_b[...] = total[8:9]


def shards(features, degrees, tile_cols, tile_counts, tiles, weight, bias, cotangent):
    span_rows = features.shape[0]
    core = lax.axis_index("c")
    zh = lax.axis_index("zh")
    y = lax.axis_index("y")
    rep_index = zh * 4 + y
    own_degrees = lax.dynamic_slice_in_dim(degrees, rep_index * span_rows, span_rows)
    own_inv = lax.rsqrt(own_degrees.astype(jnp.float32))[:, None]
    scaled = (features.astype(jnp.float32) * own_inv).astype(jnp.bfloat16)
    inv_wide = jnp.broadcast_to(own_inv, (span_rows, F))

    moved = lax.ppermute(scaled, AXES, shard_moves())
    along_z = exchange(repeat(moved, 4), "zl").reshape(4 * span_rows, F)
    own = exchange(repeat(along_z, 4), "x").reshape(16 * span_rows, F)
    other = lax.ppermute(own, "c", [(0, 1), (1, 0)])

    group = rep_index
    place = jnp.stack(
        [core, (group // 2 + 2 + group % 4) % 4, (group % 2) ^ (group // 4)]
    ).astype(jnp.int32)
    partial = pl.pallas_call(
        gather_kernel,
        grid_spec=pltpu.PrefetchScalarGridSpec(
            num_scalar_prefetch=3,
            grid=(16,),
            in_specs=[
                pl.BlockSpec((1, 4, 4, TILE, TILE), lambda b, *_: (b, 0, 0, 0, 0)),
                pl.BlockSpec((4096, F), lambda b, *_: (0, 0)),
                pl.BlockSpec((4096, F), lambda b, *_: (0, 0)),
            ],
            out_specs=pl.BlockSpec((1, TILE, F), lambda b, *_: (b, 0, 0)),
        ),
        out_shape=jax.ShapeDtypeStruct((16, TILE, F), jnp.float32),
        compiler_params=PARAMS,
        name="aggregate",
    )(tile_cols.reshape(-1), tile_counts.reshape(-1), place, tiles, own, other)

    parts = exchange(partial.reshape(8, span_rows, F), REP)
    hidden, grads = pl.pallas_call(
        dense_kernel,
        out_shape=(
            jax.ShapeDtypeStruct((span_rows, 256), jnp.bfloat16),
            jax.ShapeDtypeStruct((16, 16, 256), jnp.float32),
        ),
        in_specs=[VMEM] * 5,
        out_specs=(VMEM, VMEM),
        compiler_params=PARAMS,
        name="dense",
    )(parts, inv_wide, weight, bias.reshape(1, 256), cotangent)

    grads = exchange(grads, FLAT)
    grads = pl.pallas_call(
        first_sum_kernel,
        out_shape=jax.ShapeDtypeStruct((16, 16, 256), jnp.float32),
        in_specs=[VMEM],
        out_specs=VMEM,
        compiler_params=PARAMS,
        name="first_sum",
    )(grads)
    grads = exchange(grads, DEEP)
    grad_w, grad_b = pl.pallas_call(
        functools.partial(last_sum_kernel, 1.0 / math.sqrt(span_rows * math.prod(SIZES))),
        out_shape=(
            jax.ShapeDtypeStruct((16, 8, 256), jnp.float32),
            jax.ShapeDtypeStruct((1, 256), jnp.float32),
        ),
        in_specs=[VMEM],
        out_specs=(VMEM, VMEM),
        compiler_params=PARAMS,
        name="last_sum",
    )(grads)
    grad_w = exchange(grad_w, FLAT).reshape(128, 256)
    return hidden, grad_w, grad_b.reshape(256)


def solution(mesh):
    fine = Mesh(mesh.devices.reshape(SIZES), AXES)
    in_specs = (
        P((ROW + REP), None),
        P(ROW),
        P(ROW, REP, None),
        P(ROW, REP),
        P(ROW, REP, None, None, None),
        P(),
        P(),
        P((ROW + REP), None),
    )
    out_specs = (P((ROW + REP), None), P(), P())
    return jax.shard_map(shards, mesh=fine, in_specs=in_specs, out_specs=out_specs, check_vma=False)
```

```python
import functools
import math

import jax
import jax.numpy as jnp
from jax import lax
from jax.experimental import pallas as pl
from jax.experimental.pallas import tpu as pltpu
from jax.sharding import Mesh, PartitionSpec as P

AXES = ("x", "zl", "c", "zh", "y")
SIZES = (4, 4, 2, 2, 4)
ROW = ("x", "zl", "c")
REP = ("zh", "y")
FLAT = ("x", "c", "y")
DEEP = ("zl", "zh")
F = 128
TILE = 128
SIDE = 4096
VMEM = pl.BlockSpec(memory_space=pltpu.VMEM)
SMEM = pl.BlockSpec(memory_space=pltpu.SMEM)
PARAMS = pltpu.CompilerParams(vmem_limit_bytes=40 * 1024 * 1024)


def flat_index(x, zl, c, zh, y):
    return (((x * 4 + zl) * 2 + c) * 2 + zh) * 4 + y


def shard_moves():
    pairs = []
    for x in range(4):
        for zl in range(4):
            for c in range(2):
                for zh in range(2):
                    for y in range(4):
                        group = x * 2 + zl // 2
                        to_x = (x + 2 + group % 4 - y) % 4
                        to_zl = 2 * ((zl // 2) ^ zh ^ (group // 4)) + zl % 2
                        pairs.append(
                            (
                                flat_index(x, zl, c, zh, y),
                                flat_index(to_x, to_zl, c, group // 4, group % 4),
                            )
                        )
    return pairs


def repeat(block, count):
    return jnp.broadcast_to(block[None], (count,) + block.shape)


def exchange(block, axes):
    return lax.all_to_all(block, axes, 0, 0, tiled=True)


def stage_kernel(cols, counts, place, tiles, start, staged, tile_list, row_list, lengths, token, sems):
    copies = [
        pltpu.make_async_copy(tiles.at[pl.ds(2 * i, 2)], staged.at[pl.ds(2 * i, 2)], sems.at[i])
        for i in range(8)
    ]
    for copy in copies:
        copy.start()
    core, x0, z1 = place[0], place[1], place[2]

    def list_block(block, carry):
        length = jnp.int32(0)
        for side in range(2):
            for z0 in range(2):
                slab = z0 * 2 + (core ^ side)
                live = counts[slab, block]
                for k in range(4):
                    col = cols[slab, k, block]
                    at_x = (x0 - (col // 2)) & 3
                    at_z = (z1 ^ (col >> 3)) * 2 + z0
                    row = ((at_x * 4 + at_z) * 2 + (col & 1)) * TILE
                    tile_list[block * 16 + length] = slab * 4 + k
                    row_list[block * 16 + length] = row + side * SIDE
                    length = length + jnp.where(k < live, 1, 0)
        lengths[block] = length
        return carry

    lax.fori_loop(0, 16, list_block, 0)
    token[...] = start[0:8, :].astype(jnp.float32)
    for copy in copies:
        copy.wait()


def repeat_kernel(block, token, out):
    for i in range(out.shape[0]):
        out[i] = block[...]


STEPS = (2, 3, 4, 5, 6, 8)


def gather_kernel(tile_list, row_list, lengths, tiles, own, other, out):
    def products(block, length, pairs, sure):
        total = jnp.zeros((TILE, F), jnp.float32)
        for pair in range(pairs):
            picks, chosen = [], []
            for slot in (2 * pair, 2 * pair + 1):
                at = slot if slot < sure else jnp.minimum(slot, length - 1)
                row = row_list[block * 16 + at]
                begin = pl.multiple_of(row & (SIDE - 1), TILE)
                pick = jnp.where(
                    row >= SIDE, other[pl.ds(begin, TILE), :], own[pl.ds(begin, TILE), :]
                )
                if slot >= sure:
                    pick = jnp.where(slot < length, pick, jnp.zeros_like(pick))
                picks.append(pick)
                chosen.append(tiles[block, tile_list[block * 16 + at]])
            total += jnp.dot(
                jnp.concatenate(chosen, axis=1),
                jnp.concatenate(picks, axis=0),
                preferred_element_type=jnp.float32,
            )
        out[block] = total.astype(out.dtype)

    def one_block(block, carry):
        length = lengths[block]
        sure = 4
        for pairs in STEPS:
            low = sure if pairs > STEPS[0] else 0

            @pl.when((length > low) & (length <= 2 * pairs))
            def _(pairs=pairs, sure=sure if pairs == STEPS[0] else sure + 1):
                products(block, length, pairs, sure)

            sure = 2 * pairs
        return carry

    lax.fori_loop(0, 16, one_block, 0)


def dense_kernel(parts, inv, weight, bias, cotangent, hidden, grads):
    summed = parts[0].astype(jnp.float32)
    for i in range(1, 8):
        summed += parts[i].astype(jnp.float32)
    aggregated = (summed * inv[...]).astype(jnp.bfloat16)
    pre_act = jnp.dot(aggregated, weight[...], preferred_element_type=jnp.float32) + bias[...]
    sig = 1.0 / (1.0 + jnp.exp(-pre_act))
    hidden[...] = (pre_act * sig).astype(jnp.bfloat16)
    pre_grad = (
        cotangent[...].astype(jnp.float32) * sig * (1.0 + pre_act * (1.0 - sig))
    ).astype(jnp.bfloat16)
    grad_w = lax.dot_general(
        aggregated, pre_grad, (((0,), (0,)), ((), ())), preferred_element_type=jnp.float32
    )
    grad_b = jnp.sum(pre_grad.astype(jnp.float32), axis=0, keepdims=True)
    grad_b = jnp.concatenate([grad_b[:, :128], grad_b[:, 128:]] * 2, axis=0)
    for i in range(32):
        grads[i] = jnp.concatenate([grad_w[i * 4 : i * 4 + 4], grad_b], axis=1)


def add_up(parts, count):
    terms = [parts[i] for i in range(count)]
    while len(terms) > 1:
        terms = [a + b for a, b in zip(terms[::2], terms[1::2])]
    return terms[0]


def first_sum_kernel(parts, out):
    total = add_up(parts, 32)
    for i in range(8):
        out[i] = total


def last_sum_kernel(scale, parts, grad_w, grad_b):
    total = add_up(parts, 8) * scale
    for i in range(32):
        grad_w[i] = total[:, 0:256]
    grad_b[...] = jnp.concatenate([total[0:1, 256:384], total[1:2, 256:384]], axis=1)


def join_kernel(chunks, out):
    for i in range(16):
        out[i * 8 : i * 8 + 8] = jnp.concatenate([chunks[2 * i], chunks[2 * i + 1]], axis=0)


def shards(features, degrees, tile_cols, tile_counts, tiles, weight, bias, cotangent):
    span_rows = features.shape[0]
    core = lax.axis_index("c")
    zh = lax.axis_index("zh")
    y = lax.axis_index("y")
    rep_index = zh * 4 + y
    own_degrees = lax.dynamic_slice_in_dim(degrees, rep_index * span_rows, span_rows)
    own_inv = lax.rsqrt(own_degrees.astype(jnp.float32))[:, None]
    scaled = (features.astype(jnp.float32) * own_inv).astype(jnp.bfloat16)
    inv_wide = jnp.broadcast_to(own_inv, (span_rows, F))

    group = rep_index
    place = jnp.stack(
        [core, (group // 2 + 2 + group % 4) % 4, (group % 2) ^ (group // 4)]
    ).astype(jnp.int32)
    moved = lax.ppermute(scaled, AXES, shard_moves())
    staged, tile_list, row_list, lengths, token = pl.pallas_call(
        stage_kernel,
        out_shape=(
            jax.ShapeDtypeStruct((16, 16, TILE, TILE), tiles.dtype),
            jax.ShapeDtypeStruct((256,), jnp.int32),
            jax.ShapeDtypeStruct((256,), jnp.int32),
            jax.ShapeDtypeStruct((16,), jnp.int32),
            jax.ShapeDtypeStruct((8, F), jnp.float32),
        ),
        in_specs=[SMEM, SMEM, SMEM, pl.BlockSpec(memory_space=pl.ANY), VMEM],
        out_specs=(VMEM, SMEM, SMEM, SMEM, VMEM),
        scratch_shapes=[pltpu.SemaphoreType.DMA((8,))],
        compiler_params=PARAMS,
        cost_estimate=pl.CostEstimate(flops=0, bytes_accessed=16 * 2**20, transcendentals=0),
        name="stage",
    )(
        tile_cols.transpose(1, 2, 0),
        tile_counts.T,
        place,
        tiles.reshape(16, 16, TILE, TILE),
        scaled,
    )
    repeated = pl.pallas_call(
        repeat_kernel,
        out_shape=jax.ShapeDtypeStruct((4, span_rows, F), jnp.bfloat16),
        in_specs=[VMEM, VMEM],
        out_specs=VMEM,
        compiler_params=PARAMS,
        name="repeat",
    )(moved, token)
    along_z = exchange(repeated, "zl").reshape(4 * span_rows, F)
    own = exchange(repeat(along_z, 4), "x").reshape(16 * span_rows, F)
    other = lax.ppermute(own, "c", [(0, 1), (1, 0)])

    partial = pl.pallas_call(
        gather_kernel,
        in_specs=[SMEM, SMEM, SMEM, VMEM, VMEM, VMEM],
        out_specs=VMEM,
        out_shape=jax.ShapeDtypeStruct((16, TILE, F), jnp.bfloat16),
        compiler_params=PARAMS,
        name="aggregate",
    )(tile_list, row_list, lengths, staged, own, other)

    parts = exchange(partial.reshape(8, span_rows, F), REP)
    hidden, grads = pl.pallas_call(
        dense_kernel,
        out_shape=(
            jax.ShapeDtypeStruct((span_rows, 256), jnp.bfloat16),
            jax.ShapeDtypeStruct((32, 4, 384), jnp.float32),
        ),
        in_specs=[VMEM] * 5,
        out_specs=(VMEM, VMEM),
        compiler_params=PARAMS,
        name="dense",
    )(parts, inv_wide, weight, bias.reshape(1, 256), cotangent)

    grads = exchange(grads, FLAT)
    grads = pl.pallas_call(
        first_sum_kernel,
        out_shape=jax.ShapeDtypeStruct((8, 4, 384), jnp.float32),
        in_specs=[VMEM],
        out_specs=VMEM,
        compiler_params=PARAMS,
        name="first_sum",
    )(grads)
    grads = exchange(grads, DEEP)
    grad_w, grad_b = pl.pallas_call(
        functools.partial(last_sum_kernel, 1.0 / math.sqrt(span_rows * math.prod(SIZES))),
        out_shape=(
            jax.ShapeDtypeStruct((32, 4, 256), jnp.float32),
            jax.ShapeDtypeStruct((1, 256), jnp.float32),
        ),
        in_specs=[VMEM],
        out_specs=(VMEM, VMEM),
        compiler_params=PARAMS,
        name="last_sum",
    )(grads)
    grad_w = pl.pallas_call(
        join_kernel,
        out_shape=jax.ShapeDtypeStruct((128, 256), jnp.float32),
        in_specs=[VMEM],
        out_specs=VMEM,
        compiler_params=PARAMS,
        name="join",
    )(exchange(grad_w, FLAT))
    return hidden, grad_w, grad_b.reshape(256)


def solution(mesh):
    fine = Mesh(mesh.devices.reshape(SIZES), AXES)
    in_specs = (
        P((ROW + REP), None),
        P(ROW),
        P(ROW, REP, None),
        P(ROW, REP),
        P(ROW, REP, None, None, None),
        P(),
        P(),
        P((ROW + REP), None),
    )
    out_specs = (P((ROW + REP), None), P(), P())
    return jax.shard_map(shards, mesh=fine, in_specs=in_specs, out_specs=out_specs, check_vma=False)
```

```python
import functools
import math

import jax
import jax.numpy as jnp
from jax import lax
from jax.experimental import pallas as pl
from jax.experimental.pallas import tpu as pltpu
from jax.sharding import Mesh, PartitionSpec as P

AXES = ("x", "zl", "c", "zh", "y")
SIZES = (4, 4, 2, 2, 4)
ROW = ("x", "zl", "c")
REP = ("zh", "y")
FLAT = ("x", "y")
DEEP = ("zl", "zh")
F = 128
TILE = 128
SIDE = 4096
VMEM = pl.BlockSpec(memory_space=pltpu.VMEM)
SMEM = pl.BlockSpec(memory_space=pltpu.SMEM)
PARAMS = pltpu.CompilerParams(vmem_limit_bytes=40 * 1024 * 1024)


def flat_index(x, zl, c, zh, y):
    return (((x * 4 + zl) * 2 + c) * 2 + zh) * 4 + y


def shard_moves():
    pairs = []
    for x in range(4):
        for zl in range(4):
            for c in range(2):
                for zh in range(2):
                    for y in range(4):
                        group = x * 2 + zl // 2
                        to_x = (x + 2 + group % 4 - y) % 4
                        to_zl = 2 * ((zl // 2) ^ zh ^ (group // 4)) + zl % 2
                        pairs.append(
                            (
                                flat_index(x, zl, c, zh, y),
                                flat_index(to_x, to_zl, c, group // 4, group % 4),
                            )
                        )
    return pairs


def repeat(block, count):
    return jnp.broadcast_to(block[None], (count,) + block.shape)


def exchange(block, axes):
    return lax.all_to_all(block, axes, 0, 0, tiled=True)


def scale_kernel(degrees, features, scaled, inv):
    share = lax.axis_index("zh") * 4 + lax.axis_index("y")
    for half in range(2):
        own = degrees[pl.ds(share * 2 + half, 1), :].astype(jnp.float32)
        wide = jnp.broadcast_to(lax.rsqrt(own), (TILE, F)).T
        rows = pl.ds(half * TILE, TILE)
        inv[rows, :] = wide
        scaled[rows, :] = (features[rows, :].astype(jnp.float32) * wide).astype(jnp.bfloat16)


def stage_kernel(tiles, start, staged, token, sems):
    copies = [
        pltpu.make_async_copy(tiles.at[i], staged.at[i], sems.at[i]) for i in range(16)
    ]
    for copy in copies:
        copy.start()
    token[...] = start[...]
    for copy in copies:
        copy.wait()


def list_kernel(cols, counts, after, lists):
    core, zh, y = lax.axis_index("c"), lax.axis_index("zh"), lax.axis_index("y")
    x0 = zh * 2 + (y >> 1) + 2 + y
    z1 = (y & 1) ^ zh
    length = jnp.zeros((1, 16), jnp.int32)
    rows = lax.broadcasted_iota(jnp.int32, (24, 16), 0)
    total = jnp.zeros((24, 16), jnp.int32)
    for slab in range(4):
        for k in range(4):
            col = cols[slab, k : k + 1, :]
            at_x = (x0 - (col >> 1)) & 3
            at_z = ((z1 ^ (col >> 3)) << 1) + slab // 2
            code = ((at_x * 4 + at_z) * 2 + (col & 1)) * TILE
            code += ((core ^ slab) & 1) * SIDE + (slab * 4 + k) * (2 * SIDE)
            live = counts[slab : slab + 1, :] > k
            total += jnp.where((rows == length) & live, code, 0)
            length += live.astype(jnp.int32)
    lists[...] = jnp.where(rows == 16, length, total)


def repeat_kernel(block, token, out):
    for i in range(out.shape[0]):
        out[i] = block[...]


STEPS = (2, 3, 4, 5, 6, 8)


def gather_kernel(lists, tiles, own, other, out):
    def products(block, length, pairs, sure):
        total = jnp.zeros((TILE, F), jnp.float32)
        for pair in range(pairs):
            picks, chosen = [], []
            for slot in (2 * pair, 2 * pair + 1):
                at = slot if slot < sure else jnp.minimum(slot, length - 1)
                code = lists[at, block]
                begin = pl.multiple_of(code & (SIDE - 1), TILE)
                pick = jnp.where(
                    (code & SIDE) > 0, other[pl.ds(begin, TILE), :], own[pl.ds(begin, TILE), :]
                )
                if slot >= sure:
                    pick = jnp.where(slot < length, pick, jnp.zeros_like(pick))
                picks.append(pick)
                chosen.append(tiles[block, code >> 13])
            total += jnp.dot(
                jnp.concatenate(chosen, axis=1),
                jnp.concatenate(picks, axis=0),
                preferred_element_type=jnp.float32,
            )
        out[(block >> 1) & 3, block >> 3, block & 1] = total.astype(out.dtype)

    def one_block(block, carry):
        length = lists[16, block]
        sure = 4
        for pairs in STEPS:
            low = sure if pairs > STEPS[0] else 0

            @pl.when((length > low) & (length <= 2 * pairs))
            def _(pairs=pairs, sure=sure if pairs == STEPS[0] else sure + 1):
                products(block, length, pairs, sure)

            sure = 2 * pairs
        return carry

    lax.fori_loop(0, 16, one_block, 0)


def far_sum_kernel(parts, out):
    far = 1 - lax.axis_index("zh")
    out[...] = add_up([parts[i, far].astype(jnp.float32) for i in range(4)], 4).astype(out.dtype)


def dense_kernel(parts, far, inv, weight, bias, cotangent, hidden, grads):
    near = lax.axis_index("zh")
    summed = add_up([parts[i, near].astype(jnp.float32) for i in range(4)], 4)
    summed += far[...].astype(jnp.float32)
    aggregated = (summed * inv[...]).astype(jnp.bfloat16)
    pre_act = jnp.dot(aggregated, weight[...], preferred_element_type=jnp.float32) + bias[...]
    sig = 1.0 / (1.0 + jnp.exp(-pre_act))
    hidden[...] = (pre_act * sig).astype(jnp.bfloat16)
    pre_grad = (
        cotangent[...].astype(jnp.float32) * sig * (1.0 + pre_act * (1.0 - sig))
    ).astype(jnp.bfloat16)
    grad_w = lax.dot_general(
        aggregated, pre_grad, (((0,), (0,)), ((), ())), preferred_element_type=jnp.float32
    )
    grad_b = jnp.sum(pre_grad.astype(jnp.float32), axis=0, keepdims=True)
    grad_b = jnp.concatenate([grad_b[:, :128], grad_b[:, 128:]] * 4, axis=0)
    for i in range(16):
        grads[i] = jnp.concatenate([grad_w[i * 8 : i * 8 + 8], grad_b], axis=1)


def add_up(parts, count):
    terms = [parts[i] for i in range(count)]
    while len(terms) > 1:
        terms = [a + b for a, b in zip(terms[::2], terms[1::2])]
    return terms[0]


def first_sum_kernel(parts, out):
    out[...] = add_up(parts, 16)


def pair_sum_kernel(mine, theirs, out):
    total = mine[...] + theirs[...]
    for i in range(8):
        out[i] = total


def last_sum_kernel(scale, parts, grad_w, grad_b):
    total = add_up(parts, 8) * scale
    for i in range(16):
        grad_w[i] = total[:, 0:256]
    grad_b[...] = jnp.concatenate([total[0:1, 256:384], total[1:2, 256:384]], axis=1)


def shards(features, degrees, tile_cols, tile_counts, tiles, weight, bias, cotangent):
    span_rows = features.shape[0]
    core = lax.axis_index("c")
    zh = lax.axis_index("zh")
    y = lax.axis_index("y")
    rep_index = zh * 4 + y
    scaled, inv_wide = pl.pallas_call(
        scale_kernel,
        out_shape=(
            jax.ShapeDtypeStruct((span_rows, F), jnp.bfloat16),
            jax.ShapeDtypeStruct((span_rows, F), jnp.float32),
        ),
        grid=(1,),
        in_specs=[
            pl.BlockSpec((16, TILE), lambda i: (0, 0)),
            pl.BlockSpec((span_rows, F), lambda i: (0, 0)),
        ],
        out_specs=(VMEM, VMEM),
        compiler_params=PARAMS,
        name="scale",
    )(degrees.reshape(16, TILE), features)

    moved = lax.ppermute(scaled, AXES, shard_moves())
    staged, token = pl.pallas_call(
        stage_kernel,
        out_shape=(
            jax.ShapeDtypeStruct((16, 16, TILE, TILE), tiles.dtype),
            jax.ShapeDtypeStruct((8, F), jnp.float32),
        ),
        grid=(1,),
        in_specs=[
            pl.BlockSpec(memory_space=pl.ANY),
            pl.BlockSpec((8, F), lambda i: (0, 0)),
        ],
        out_specs=(VMEM, VMEM),
        scratch_shapes=[pltpu.SemaphoreType.DMA((16,))],
        compiler_params=PARAMS,
        cost_estimate=pl.CostEstimate(flops=0, bytes_accessed=16 * 2**20, transcendentals=0),
        name="stage",
    )(tiles.reshape(16, 16, TILE, TILE), inv_wide)
    repeated = pl.pallas_call(
        repeat_kernel,
        out_shape=jax.ShapeDtypeStruct((4, span_rows, F), jnp.bfloat16),
        in_specs=[VMEM, VMEM],
        out_specs=VMEM,
        compiler_params=PARAMS,
        name="repeat",
    )(moved, token)
    along_z = exchange(repeated, "zl").reshape(4 * span_rows, F)
    own = exchange(repeat(along_z, 4), "x").reshape(16 * span_rows, F)
    other = lax.ppermute(own, "c", [(0, 1), (1, 0)])

    lists = pl.pallas_call(
        list_kernel,
        out_shape=jax.ShapeDtypeStruct((24, 16), jnp.int32),
        grid=(1,),
        in_specs=[
            pl.BlockSpec((4, 4, 16), lambda i: (0, 0, 0)),
            pl.BlockSpec((4, 16), lambda i: (0, 0)),
            pl.BlockSpec(memory_space=pl.ANY),
        ],
        out_specs=pl.BlockSpec((24, 16), lambda i: (0, 0)),
        compiler_params=PARAMS,
        name="list",
    )(tile_cols.transpose(1, 2, 0), tile_counts.T, own)
    partial = pl.pallas_call(
        gather_kernel,
        in_specs=[SMEM, VMEM, VMEM, VMEM],
        out_specs=VMEM,
        out_shape=jax.ShapeDtypeStruct((4, 2, 2, TILE, F), jnp.bfloat16),
        compiler_params=PARAMS,
        name="aggregate",
    )(lists, staged, own, other)

    parts = exchange(partial.reshape(4, 2, span_rows, F), "y")
    far = pl.pallas_call(
        far_sum_kernel,
        out_shape=jax.ShapeDtypeStruct((span_rows, F), jnp.bfloat16),
        in_specs=[VMEM],
        out_specs=VMEM,
        compiler_params=PARAMS,
        name="far_sum",
    )(parts)
    far = lax.ppermute(far, "zh", [(0, 1), (1, 0)])
    hidden, grads = pl.pallas_call(
        dense_kernel,
        out_shape=(
            jax.ShapeDtypeStruct((span_rows, 256), jnp.bfloat16),
            jax.ShapeDtypeStruct((16, 8, 384), jnp.float32),
        ),
        in_specs=[VMEM] * 6,
        out_specs=(VMEM, VMEM),
        compiler_params=PARAMS,
        name="dense",
    )(parts, far, inv_wide, weight, bias.reshape(1, 256), cotangent)

    grads = exchange(grads, FLAT)
    grads = pl.pallas_call(
        first_sum_kernel,
        out_shape=jax.ShapeDtypeStruct((8, 384), jnp.float32),
        in_specs=[VMEM],
        out_specs=VMEM,
        compiler_params=PARAMS,
        name="first_sum",
    )(grads)
    grads = pl.pallas_call(
        pair_sum_kernel,
        out_shape=jax.ShapeDtypeStruct((8, 8, 384), jnp.float32),
        in_specs=[VMEM, VMEM],
        out_specs=VMEM,
        compiler_params=PARAMS,
        name="pair_sum",
    )(grads, lax.ppermute(grads, "c", [(0, 1), (1, 0)]))
    grads = exchange(grads, DEEP)
    grad_w, grad_b = pl.pallas_call(
        functools.partial(last_sum_kernel, 1.0 / math.sqrt(span_rows * math.prod(SIZES))),
        out_shape=(
            jax.ShapeDtypeStruct((16, 8, 256), jnp.float32),
            jax.ShapeDtypeStruct((1, 256), jnp.float32),
        ),
        in_specs=[VMEM],
        out_specs=(VMEM, VMEM),
        compiler_params=PARAMS,
        name="last_sum",
    )(grads)
    grad_w = exchange(grad_w, FLAT).reshape(128, 256)
    return hidden, grad_w, grad_b.reshape(256)


def solution(mesh):
    fine = Mesh(mesh.devices.reshape(SIZES), AXES)
    in_specs = (
        P((ROW + REP), None),
        P(ROW),
        P(ROW, REP, None),
        P(ROW, REP),
        P(ROW, REP, None, None, None),
        P(),
        P(),
        P((ROW + REP), None),
    )
    out_specs = (P((ROW + REP), None), P(), P())
    return jax.shard_map(shards, mesh=fine, in_specs=in_specs, out_specs=out_specs, check_vma=False)
```

```python
import functools
import math

import jax
import jax.numpy as jnp
from jax import lax
from jax.experimental import pallas as pl
from jax.experimental.pallas import tpu as pltpu
from jax.sharding import Mesh, PartitionSpec as P

AXES = ("x", "zl", "c", "zh", "y")
SIZES = (4, 4, 2, 2, 4)
ROW = ("x", "zl", "c")
REP = ("zh", "y")
FLAT = ("x", "y")
DEEP = ("zl", "zh")
F = 128
TILE = 128
SIDE = 4096
VMEM = pl.BlockSpec(memory_space=pltpu.VMEM)
SMEM = pl.BlockSpec(memory_space=pltpu.SMEM)
PARAMS = pltpu.CompilerParams(vmem_limit_bytes=40 * 1024 * 1024)


COST = pl.CostEstimate(flops=2**30, bytes_accessed=2**23, transcendentals=0)


def flat_index(x, zl, c, zh, y):
    return (((x * 4 + zl) * 2 + c) * 2 + zh) * 4 + y


def shard_moves():
    pairs = []
    for x in range(4):
        for zl in range(4):
            for c in range(2):
                for zh in range(2):
                    for y in range(4):
                        group = x * 2 + zl // 2
                        to_x = (x + 2 + group % 4 - y) % 4
                        to_zl = 2 * ((zl // 2) ^ zh ^ (group // 4)) + zl % 2
                        pairs.append(
                            (
                                flat_index(x, zl, c, zh, y),
                                flat_index(to_x, to_zl, c, group // 4, group % 4),
                            )
                        )
    return pairs


def repeat(block, count):
    return jnp.broadcast_to(block[None], (count,) + block.shape)


def exchange(block, axes):
    return lax.all_to_all(block, axes, 0, 0, tiled=True)


def scale_kernel(degrees, features, scaled, inv):
    share = lax.axis_index("zh") * 4 + lax.axis_index("y")
    for half in range(2):
        own = degrees[pl.ds(share * 2 + half, 1), :].astype(jnp.float32)
        wide = jnp.broadcast_to(lax.rsqrt(own), (TILE, F)).T
        rows = pl.ds(half * TILE, TILE)
        inv[rows, :] = wide
        scaled[rows, :] = (features[rows, :].astype(jnp.float32) * wide).astype(jnp.bfloat16)


def stage_kernel(tiles, start, staged, token, sems):
    copies = [
        pltpu.make_async_copy(tiles.at[i], staged.at[i], sems.at[i]) for i in range(16)
    ]
    for copy in copies:
        copy.start()
    token[...] = start[...]
    for copy in copies:
        copy.wait()


def repeat_kernel(block, token, out):
    for i in range(out.shape[0]):
        out[i] = block[...]


def list_kernel(cols, counts, after, lists):
    core, zh, y = lax.axis_index("c"), lax.axis_index("zh"), lax.axis_index("y")
    x0 = zh * 2 + (y >> 1) + 2 + y
    z1 = (y & 1) ^ zh
    rows = lax.broadcasted_iota(jnp.int32, (24, 16), 0)
    total = jnp.zeros((24, 16), jnp.int32)
    lengths = [jnp.zeros((1, 16), jnp.int32) for _ in range(2)]
    for slab in range(4):
        side = (core ^ slab) & 1
        for k in range(4):
            col = cols[slab, k : k + 1, :]
            at_x = (lax.axis_index("x") - x0 + (col >> 1)) & 3
            at_z = ((z1 ^ (col >> 3)) << 1) + slab // 2
            code = ((at_x * 4 + at_z) * 2 + (col & 1)) * TILE + (slab * 4 + k) * SIDE
            live = counts[slab : slab + 1, :] > k
            length = jnp.where(side == 0, lengths[0], lengths[1] + 8)
            total += jnp.where((rows == length) & live, code, 0)
            lengths = [
                lengths[i] + jnp.where(live & (side == i), 1, 0) for i in range(2)
            ]
    total = jnp.where(rows == 16, lengths[0], total)
    lists[...] = jnp.where(rows == 17, lengths[1], total)


def half_products(side, lists, tiles, feats, use, count, first_of):
    def one(block, pairs):
        length = lists[16 + side, block]
        total = jnp.zeros((TILE, F), jnp.float32)
        for pair in range(pairs):
            picks, chosen = [], []
            for slot in (2 * pair, 2 * pair + 1):
                at = slot if slot < 2 else jnp.minimum(slot, length - 1)
                code = lists[8 * side + at, block]
                begin = pl.multiple_of(code & (SIDE - 1), TILE)
                pick = feats[pl.ds(begin, TILE), :]
                if slot >= 2:
                    pick = jnp.where(slot < length, pick, jnp.zeros_like(pick))
                picks.append(pick)
                chosen.append(tiles[block, code >> 12])
            total += jnp.dot(
                jnp.concatenate(chosen, axis=1),
                jnp.concatenate(picks, axis=0),
                preferred_element_type=jnp.float32,
            )
        use(block, total)

    def two(first):
        length = jnp.maximum(lists[16 + side, first], lists[16 + side, first + 1])
        for pairs in range(1, 5):

            @pl.when((length + 1) >> 1 == pairs)
            def _(pairs=pairs):
                one(first, pairs)
                one(first + 1, pairs)

    lax.fori_loop(0, count, lambda step, _: two(first_of(step)), None)


def join(parts, feats):
    for i, part in enumerate(parts):
        feats[i * 1024 : (i + 1) * 1024, :] = part[...]


def own_kernel(lists, tiles, a, b, c, d, out, feats):
    join((a, b, c, d), feats)

    def use(block, total):
        out[block] = total

    half_products(0, lists, tiles, feats, use, 8, lambda step: step * 2)


def other_kernel(shifts, lists, tiles, a, b, c, d, begun, *refs):
    feats = refs[-1]
    join((a, b, c, d), feats)
    for shift, out in zip(shifts, refs[-1 - len(shifts) : -1]):
        share = (lax.axis_index("y") + shift) & 3

        def use(block, total, out=out):
            out[block >> 3, block & 1] = (total + begun[block]).astype(out.dtype)

        half_products(1, lists, tiles, feats, use, 2, lambda step: step * 8 + share * 2)


def add_up(parts, count):
    terms = [parts[i] for i in range(count)]
    while len(terms) > 1:
        terms = [a + b for a, b in zip(terms[::2], terms[1::2])]
    return terms[0]


def far_sum_kernel(a, b, c, d, out):
    far = 1 - lax.axis_index("zh")
    out[...] = add_up([r[far].astype(jnp.float32) for r in (a, b, c, d)], 4).astype(out.dtype)


def dense_kernel(a, b, c, d, far, inv, weight, bias, cotangent, hidden, grads):
    near = lax.axis_index("zh")
    summed = add_up([r[near].astype(jnp.float32) for r in (a, b, c, d)], 4)
    summed += far[...].astype(jnp.float32)
    aggregated = (summed * inv[...]).astype(jnp.bfloat16)
    pre_act = jnp.dot(aggregated, weight[...], preferred_element_type=jnp.float32) + bias[...]
    sig = 1.0 / (1.0 + jnp.exp(-pre_act))
    hidden[...] = (pre_act * sig).astype(jnp.bfloat16)
    pre_grad = (
        cotangent[...].astype(jnp.float32) * sig * (1.0 + pre_act * (1.0 - sig))
    ).astype(jnp.bfloat16)
    grad_w = lax.dot_general(
        aggregated, pre_grad, (((0,), (0,)), ((), ())), preferred_element_type=jnp.float32
    )
    grad_b = jnp.sum(pre_grad.astype(jnp.float32), axis=0, keepdims=True)
    grad_b = jnp.concatenate([grad_b[:, :128], grad_b[:, 128:]] * 4, axis=0)
    for i in range(16):
        grads[i] = jnp.concatenate([grad_w[i * 8 : i * 8 + 8], grad_b], axis=1)


def first_sum_kernel(parts, out):
    out[...] = add_up(parts, 16)


def pair_sum_kernel(mine, theirs, out):
    total = mine[...] + theirs[...]
    for i in range(8):
        out[i] = total


def last_sum_kernel(scale, parts, grad_w, grad_b):
    total = add_up(parts, 8) * scale
    for i in range(16):
        grad_w[i] = total[:, 0:256]
    grad_b[...] = jnp.concatenate([total[0:1, 256:384], total[1:2, 256:384]], axis=1)


def shards(features, degrees, tile_cols, tile_counts, tiles, weight, bias, cotangent):
    span_rows = features.shape[0]
    core = lax.axis_index("c")
    zh = lax.axis_index("zh")
    y = lax.axis_index("y")
    rep_index = zh * 4 + y
    scaled, inv_wide = pl.pallas_call(
        scale_kernel,
        out_shape=(
            jax.ShapeDtypeStruct((span_rows, F), jnp.bfloat16),
            jax.ShapeDtypeStruct((span_rows, F), jnp.float32),
        ),
        grid=(1,),
        in_specs=[
            pl.BlockSpec((16, TILE), lambda i: (0, 0)),
            pl.BlockSpec((span_rows, F), lambda i: (0, 0)),
        ],
        out_specs=(VMEM, VMEM),
        compiler_params=PARAMS,
        name="scale",
    )(degrees.reshape(16, TILE), features)

    moved = lax.ppermute(scaled, AXES, shard_moves())
    staged, token = pl.pallas_call(
        stage_kernel,
        out_shape=(
            jax.ShapeDtypeStruct((16, 16, TILE, TILE), tiles.dtype),
            jax.ShapeDtypeStruct((8, F), jnp.float32),
        ),
        grid=(1,),
        in_specs=[
            pl.BlockSpec(memory_space=pl.ANY),
            pl.BlockSpec((8, F), lambda i: (0, 0)),
        ],
        out_specs=(VMEM, VMEM),
        scratch_shapes=[pltpu.SemaphoreType.DMA((16,))],
        compiler_params=PARAMS,
        cost_estimate=pl.CostEstimate(flops=0, bytes_accessed=16 * 2**20, transcendentals=0),
        name="stage",
    )(tiles.reshape(16, 16, TILE, TILE), inv_wide)
    repeated = pl.pallas_call(
        repeat_kernel,
        out_shape=jax.ShapeDtypeStruct((4, span_rows, F), jnp.bfloat16),
        in_specs=[VMEM, VMEM],
        out_specs=VMEM,
        compiler_params=PARAMS,
        name="repeat",
    )(moved, token)
    along_z = exchange(repeated, "zl").reshape(4 * span_rows, F)
    own = [along_z] + [
        lax.ppermute(along_z, "x", [(i, (i + shift) % 4) for i in range(4)]) for shift in (2, 1, 3)
    ]
    own = [own[0], own[2], own[1], own[3]]
    other = [lax.ppermute(part, "c", [(0, 1), (1, 0)]) for part in own]
    lists = pl.pallas_call(
        list_kernel,
        out_shape=jax.ShapeDtypeStruct((24, 16), jnp.int32),
        grid=(1,),
        in_specs=[
            pl.BlockSpec((4, 4, 16), lambda i: (0, 0, 0)),
            pl.BlockSpec((4, 16), lambda i: (0, 0)),
            pl.BlockSpec(memory_space=pl.ANY),
        ],
        out_specs=pl.BlockSpec((24, 16), lambda i: (0, 0)),
        compiler_params=PARAMS,
        name="list",
    )(tile_cols.transpose(1, 2, 0), tile_counts.T, own[3])
    begun = pl.pallas_call(
        own_kernel,
        in_specs=[SMEM] + [VMEM] * 5,
        out_specs=VMEM,
        out_shape=jax.ShapeDtypeStruct((16, TILE, F), jnp.float32),
        scratch_shapes=[pltpu.VMEM((SIDE, F), jnp.bfloat16)],
        compiler_params=PARAMS,
        cost_estimate=COST,
        name="own_half",
    )(lists, staged, *own)
    def other_half(shifts, after):
        parts = pl.pallas_call(
            functools.partial(other_kernel, shifts),
            in_specs=[SMEM] + [VMEM] * 6 + [pl.BlockSpec(memory_space=pl.ANY)] * len(after),
            out_specs=[VMEM] * len(shifts),
            scratch_shapes=[pltpu.VMEM((SIDE, F), jnp.bfloat16)],
            out_shape=[jax.ShapeDtypeStruct((2, 2, TILE, F), jnp.bfloat16)] * len(shifts),
            compiler_params=PARAMS,
            cost_estimate=COST,
            name="other_half",
        )(lists, staged, *other, begun, *after)
        return [part.reshape(2, span_rows, F) for part in parts]

    sent = other_half((2, 1, 3), ())
    parts = [
        lax.ppermute(part, "y", [(i, (i + shift) % 4) for i in range(4)])
        for part, shift in zip(sent, (2, 1, 3))
    ] + other_half((0,), sent[:1])
    far = pl.pallas_call(
        far_sum_kernel,
        out_shape=jax.ShapeDtypeStruct((span_rows, F), jnp.bfloat16),
        in_specs=[VMEM] * 4,
        out_specs=VMEM,
        compiler_params=PARAMS,
        name="far_sum",
    )(*parts)
    far = lax.ppermute(far, "zh", [(0, 1), (1, 0)])
    hidden, grads = pl.pallas_call(
        dense_kernel,
        out_shape=(
            jax.ShapeDtypeStruct((span_rows, 256), jnp.bfloat16),
            jax.ShapeDtypeStruct((16, 8, 384), jnp.float32),
        ),
        in_specs=[VMEM] * 9,
        out_specs=(VMEM, VMEM),
        compiler_params=PARAMS,
        name="dense",
    )(*parts, far, inv_wide, weight, bias.reshape(1, 256), cotangent)

    grads = exchange(grads, FLAT)
    grads = pl.pallas_call(
        first_sum_kernel,
        out_shape=jax.ShapeDtypeStruct((8, 384), jnp.float32),
        in_specs=[VMEM],
        out_specs=VMEM,
        compiler_params=PARAMS,
        name="first_sum",
    )(grads)
    grads = pl.pallas_call(
        pair_sum_kernel,
        out_shape=jax.ShapeDtypeStruct((8, 8, 384), jnp.float32),
        in_specs=[VMEM, VMEM],
        out_specs=VMEM,
        compiler_params=PARAMS,
        name="pair_sum",
    )(grads, lax.ppermute(grads, "c", [(0, 1), (1, 0)]))
    grads = exchange(grads, DEEP)
    grad_w, grad_b = pl.pallas_call(
        functools.partial(last_sum_kernel, 1.0 / math.sqrt(span_rows * math.prod(SIZES))),
        out_shape=(
            jax.ShapeDtypeStruct((16, 8, 256), jnp.float32),
            jax.ShapeDtypeStruct((1, 256), jnp.float32),
        ),
        in_specs=[VMEM],
        out_specs=(VMEM, VMEM),
        compiler_params=PARAMS,
        name="last_sum",
    )(grads)
    grad_w = exchange(grad_w, FLAT).reshape(128, 256)
    return hidden, grad_w, grad_b.reshape(256)


def solution(mesh):
    fine = Mesh(mesh.devices.reshape(SIZES), AXES)
    in_specs = (
        P((ROW + REP), None),
        P(ROW),
        P(ROW, REP, None),
        P(ROW, REP),
        P(ROW, REP, None, None, None),
        P(),
        P(),
        P((ROW + REP), None),
    )
    out_specs = (P((ROW + REP), None), P(), P())
    return jax.shard_map(shards, mesh=fine, in_specs=in_specs, out_specs=out_specs, check_vma=False)
```

```python
import functools
import math

import jax
import jax.numpy as jnp
from jax import lax
from jax.experimental import pallas as pl
from jax.experimental.pallas import tpu as pltpu
from jax.sharding import Mesh, PartitionSpec as P

AXES = ("x", "zl", "c", "zh", "y")
SIZES = (4, 4, 2, 2, 4)
ROW = ("x", "zl", "c")
REP = ("zh", "y")
FLAT = ("x", "y")
DEEP = ("zl", "zh")
F = 128
TILE = 128
SIDE = 4096
VMEM = pl.BlockSpec(memory_space=pltpu.VMEM)
SMEM = pl.BlockSpec(memory_space=pltpu.SMEM)
PARAMS = pltpu.CompilerParams(vmem_limit_bytes=40 * 1024 * 1024)


COST = pl.CostEstimate(flops=2**30, bytes_accessed=2**23, transcendentals=0)


def flat_index(x, zl, c, zh, y):
    return (((x * 4 + zl) * 2 + c) * 2 + zh) * 4 + y


def shard_moves():
    pairs = []
    for x in range(4):
        for zl in range(4):
            for c in range(2):
                for zh in range(2):
                    for y in range(4):
                        group = x * 2 + zl // 2
                        to_x = (x + 2 + group % 4 - y) % 4
                        to_zl = 2 * ((zl // 2) ^ zh ^ (group // 4)) + zl % 2
                        pairs.append(
                            (
                                flat_index(x, zl, c, zh, y),
                                flat_index(to_x, to_zl, c, group // 4, group % 4),
                            )
                        )
    return pairs


def repeat(block, count):
    return jnp.broadcast_to(block[None], (count,) + block.shape)


def exchange(block, axes):
    return lax.all_to_all(block, axes, 0, 0, tiled=True)


def scale_kernel(own_inv, features, scaled, inv):
    for half in range(2):
        wide = jnp.broadcast_to(own_inv[half : half + 1, :], (TILE, F)).T
        rows = pl.ds(half * TILE, TILE)
        inv[rows, :] = wide
        scaled[rows, :] = (features[rows, :].astype(jnp.float32) * wide).astype(jnp.bfloat16)


def stage_kernel(tiles, start, staged, token, sems):
    copies = [
        pltpu.make_async_copy(tiles.at[i], staged.at[i], sems.at[i]) for i in range(16)
    ]
    for copy in copies:
        copy.start()
    token[...] = start[...]
    for copy in copies:
        copy.wait()


def join_kernel(a, b, c, d, token, out):
    for i, part in enumerate((a, b, c, d)):
        out[i * 256 : (i + 1) * 256, :] = part[...]


def list_kernel(cols, counts, after, lists):
    core, zh, y = lax.axis_index("c"), lax.axis_index("zh"), lax.axis_index("y")
    x0 = zh * 2 + (y >> 1) + 2 + y
    z1 = (y & 1) ^ zh
    rows = lax.broadcasted_iota(jnp.int32, (24, 16), 0)
    total = jnp.zeros((24, 16), jnp.int32)
    lengths = [jnp.zeros((1, 16), jnp.int32) for _ in range(2)]
    for slab in range(4):
        side = (core ^ slab) & 1
        for k in range(4):
            col = cols[slab, k : k + 1, :]
            at_x = (lax.axis_index("x") - x0 + (col >> 1)) & 3
            at_z = (((z1 ^ (col >> 3)) << 1) + slab // 2) ^ lax.axis_index("zl")
            code = ((at_x * 4 + at_z) * 2 + (col & 1)) * TILE + (slab * 4 + k) * SIDE
            live = counts[slab : slab + 1, :] > k
            length = jnp.where(side == 0, lengths[0], lengths[1] + 8)
            total += jnp.where((rows == length) & live, code, 0)
            lengths = [
                lengths[i] + jnp.where(live & (side == i), 1, 0) for i in range(2)
            ]
    total = jnp.where(rows == 16, lengths[0], total)
    lists[...] = jnp.where(rows == 17, lengths[1], total)


def half_products(side, lists, tiles, feats, use, count, first_of):
    def one(block, pairs):
        length = lists[16 + side, block]
        total = jnp.zeros((TILE, F), jnp.float32)
        for pair in range(pairs):
            picks, chosen = [], []
            for slot in (2 * pair, 2 * pair + 1):
                at = slot if slot < 2 else jnp.minimum(slot, length - 1)
                code = lists[8 * side + at, block]
                begin = pl.multiple_of(code & (SIDE - 1), TILE)
                pick = feats[pl.ds(begin, TILE), :]
                if slot >= 2:
                    pick = jnp.where(slot < length, pick, jnp.zeros_like(pick))
                picks.append(pick)
                chosen.append(tiles[block, code >> 12])
            total += jnp.dot(
                jnp.concatenate(chosen, axis=1),
                jnp.concatenate(picks, axis=0),
                preferred_element_type=jnp.float32,
            )
        use(block, total)

    def two(first):
        length = jnp.maximum(lists[16 + side, first], lists[16 + side, first + 1])
        for pairs in range(1, 5):

            @pl.when((length + 1) >> 1 == pairs)
            def _(pairs=pairs):
                one(first, pairs)
                one(first + 1, pairs)

    lax.fori_loop(0, count, lambda step, _: two(first_of(step)), None)


def join(parts, feats):
    for i, part in enumerate(parts):
        feats[i * 1024 : (i + 1) * 1024, :] = part[...]


def own_kernel(lists, tiles, a, b, c, d, out, feats):
    join((a, b, c, d), feats)

    def use(block, total):
        out[block] = total

    half_products(0, lists, tiles, feats, use, 8, lambda step: step * 2)


def other_kernel(shifts, lists, tiles, a, b, c, d, begun, *refs):
    feats = refs[-1]
    join((a, b, c, d), feats)
    for shift, out in zip(shifts, refs[-1 - len(shifts) : -1]):
        share = (lax.axis_index("y") + shift) & 3

        def use(block, total, out=out):
            out[block >> 3, block & 1] = (total + begun[block]).astype(out.dtype)

        half_products(1, lists, tiles, feats, use, 2, lambda step: step * 8 + share * 2)


def add_up(parts, count):
    terms = [parts[i] for i in range(count)]
    while len(terms) > 1:
        terms = [a + b for a, b in zip(terms[::2], terms[1::2])]
    return terms[0]


def far_sum_kernel(a, b, c, d, out):
    far = 1 - lax.axis_index("zh")
    out[...] = add_up([r[far].astype(jnp.float32) for r in (a, b, c, d)], 4).astype(out.dtype)


def dense_kernel(a, b, c, d, far, inv, weight, bias, cotangent, hidden, grads):
    near = lax.axis_index("zh")
    summed = add_up([r[near].astype(jnp.float32) for r in (a, b, c, d)], 4)
    summed += far[...].astype(jnp.float32)
    aggregated = (summed * inv[...]).astype(jnp.bfloat16)
    pre_act = jnp.dot(aggregated, weight[...], preferred_element_type=jnp.float32) + bias[...]
    sig = 1.0 / (1.0 + jnp.exp(-pre_act))
    hidden[...] = (pre_act * sig).astype(jnp.bfloat16)
    pre_grad = (
        cotangent[...].astype(jnp.float32) * sig * (1.0 + pre_act * (1.0 - sig))
    ).astype(jnp.bfloat16)
    grad_w = lax.dot_general(
        aggregated, pre_grad, (((0,), (0,)), ((), ())), preferred_element_type=jnp.float32
    )
    grad_b = jnp.sum(pre_grad.astype(jnp.float32), axis=0, keepdims=True)
    grad_b = jnp.concatenate([grad_b[:, :128], grad_b[:, 128:]] * 4, axis=0)
    for i in range(16):
        grads[i] = jnp.concatenate([grad_w[i * 8 : i * 8 + 8], grad_b], axis=1)


def first_sum_kernel(parts, out):
    out[...] = add_up(parts, 16)


def pair_sum_kernel(mine, theirs, out):
    total = mine[...] + theirs[...]
    for i in range(8):
        out[i] = total


def last_sum_kernel(scale, parts, grad_w, grad_b):
    total = add_up(parts, 8) * scale
    for i in range(16):
        grad_w[i] = total[:, 0:256]
    grad_b[...] = jnp.concatenate([total[0:1, 256:384], total[1:2, 256:384]], axis=1)


def shards(features, degrees, tile_cols, tile_counts, tiles, weight, bias, cotangent):
    span_rows = features.shape[0]
    core = lax.axis_index("c")
    zh = lax.axis_index("zh")
    y = lax.axis_index("y")
    rep_index = zh * 4 + y
    own_degrees = lax.dynamic_slice_in_dim(degrees, (zh * 4 + y) * span_rows, span_rows)
    own_inv = lax.rsqrt(own_degrees.astype(jnp.float32)).reshape(2, TILE)
    scaled, inv_wide = pl.pallas_call(
        scale_kernel,
        out_shape=(
            jax.ShapeDtypeStruct((span_rows, F), jnp.bfloat16),
            jax.ShapeDtypeStruct((span_rows, F), jnp.float32),
        ),
        grid=(1,),
        in_specs=[
            pl.BlockSpec((2, TILE), lambda i: (0, 0)),
            pl.BlockSpec((span_rows, F), lambda i: (0, 0)),
        ],
        out_specs=(VMEM, VMEM),
        compiler_params=PARAMS,
        name="scale",
    )(own_inv, features)

    moved = lax.ppermute(scaled, AXES, shard_moves())
    staged, token = pl.pallas_call(
        stage_kernel,
        out_shape=(
            jax.ShapeDtypeStruct((16, 16, TILE, TILE), tiles.dtype),
            jax.ShapeDtypeStruct((8, F), jnp.float32),
        ),
        grid=(1,),
        in_specs=[
            pl.BlockSpec(memory_space=pl.ANY),
            pl.BlockSpec((8, F), lambda i: (0, 0)),
        ],
        out_specs=(VMEM, VMEM),
        scratch_shapes=[pltpu.SemaphoreType.DMA((16,))],
        compiler_params=PARAMS,
        cost_estimate=pl.CostEstimate(flops=0, bytes_accessed=16 * 2**20, transcendentals=0),
        name="stage",
    )(tiles.reshape(16, 16, TILE, TILE), inv_wide)
    along_z = pl.pallas_call(
        join_kernel,
        out_shape=jax.ShapeDtypeStruct((4 * span_rows, F), jnp.bfloat16),
        in_specs=[VMEM] * 5,
        out_specs=VMEM,
        compiler_params=PARAMS,
        name="join",
    )(
        moved,
        *(lax.ppermute(moved, "zl", [(i, i ^ flip) for i in range(4)]) for flip in (1, 2, 3)),
        token,
    )
    own = {0: along_z}
    for shift in (1, 3, 2):
        own[shift] = lax.ppermute(along_z, "x", [(i, (i + shift) % 4) for i in range(4)])
    other = {shift: lax.ppermute(own[shift], "c", [(0, 1), (1, 0)]) for shift in (0, 1, 3, 2)}
    own, other = ([pieces[shift] for shift in range(4)] for pieces in (own, other))
    lists = pl.pallas_call(
        list_kernel,
        out_shape=jax.ShapeDtypeStruct((24, 16), jnp.int32),
        grid=(1,),
        in_specs=[
            pl.BlockSpec((4, 4, 16), lambda i: (0, 0, 0)),
            pl.BlockSpec((4, 16), lambda i: (0, 0)),
            pl.BlockSpec(memory_space=pl.ANY),
        ],
        out_specs=pl.BlockSpec((24, 16), lambda i: (0, 0)),
        compiler_params=PARAMS,
        name="list",
    )(tile_cols.transpose(1, 2, 0), tile_counts.T, own[3])
    begun = pl.pallas_call(
        own_kernel,
        in_specs=[SMEM] + [VMEM] * 5,
        out_specs=VMEM,
        out_shape=jax.ShapeDtypeStruct((16, TILE, F), jnp.float32),
        scratch_shapes=[pltpu.VMEM((SIDE, F), jnp.bfloat16)],
        compiler_params=PARAMS,
        cost_estimate=COST,
        name="own_half",
    )(lists, staged, *own)
    def other_half(shifts, after):
        parts = pl.pallas_call(
            functools.partial(other_kernel, shifts),
            in_specs=[SMEM] + [VMEM] * 6 + [pl.BlockSpec(memory_space=pl.ANY)] * len(after),
            out_specs=[VMEM] * len(shifts),
            scratch_shapes=[pltpu.VMEM((SIDE, F), jnp.bfloat16)],
            out_shape=[jax.ShapeDtypeStruct((2, 2, TILE, F), jnp.bfloat16)] * len(shifts),
            compiler_params=PARAMS,
            cost_estimate=COST,
            name="other_half",
        )(lists, staged, *other, begun, *after)
        return [part.reshape(2, span_rows, F) for part in parts]

    sent = other_half((2, 1, 3), ())
    parts = [
        lax.ppermute(part, "y", [(i, (i + shift) % 4) for i in range(4)])
        for part, shift in zip(sent, (2, 1, 3))
    ] + other_half((0,), sent[:1])
    far = pl.pallas_call(
        far_sum_kernel,
        out_shape=jax.ShapeDtypeStruct((span_rows, F), jnp.bfloat16),
        in_specs=[VMEM] * 4,
        out_specs=VMEM,
        compiler_params=PARAMS,
        name="far_sum",
    )(*parts)
    far = lax.ppermute(far, "zh", [(0, 1), (1, 0)])
    hidden, grads = pl.pallas_call(
        dense_kernel,
        out_shape=(
            jax.ShapeDtypeStruct((span_rows, 256), jnp.bfloat16),
            jax.ShapeDtypeStruct((16, 8, 384), jnp.float32),
        ),
        in_specs=[VMEM] * 9,
        out_specs=(VMEM, VMEM),
        compiler_params=PARAMS,
        name="dense",
    )(*parts, far, inv_wide, weight, bias.reshape(1, 256), cotangent)

    grads = exchange(grads, FLAT)
    grads = pl.pallas_call(
        first_sum_kernel,
        out_shape=jax.ShapeDtypeStruct((8, 384), jnp.float32),
        in_specs=[VMEM],
        out_specs=VMEM,
        compiler_params=PARAMS,
        name="first_sum",
    )(grads)
    grads = pl.pallas_call(
        pair_sum_kernel,
        out_shape=jax.ShapeDtypeStruct((8, 8, 384), jnp.float32),
        in_specs=[VMEM, VMEM],
        out_specs=VMEM,
        compiler_params=PARAMS,
        name="pair_sum",
    )(grads, lax.ppermute(grads, "c", [(0, 1), (1, 0)]))
    grads = exchange(grads, DEEP)
    grad_w, grad_b = pl.pallas_call(
        functools.partial(last_sum_kernel, 1.0 / math.sqrt(span_rows * math.prod(SIZES))),
        out_shape=(
            jax.ShapeDtypeStruct((16, 8, 256), jnp.float32),
            jax.ShapeDtypeStruct((1, 256), jnp.float32),
        ),
        in_specs=[VMEM],
        out_specs=(VMEM, VMEM),
        compiler_params=PARAMS,
        name="last_sum",
    )(grads)
    grad_w = exchange(grad_w, FLAT).reshape(128, 256)
    return hidden, grad_w, grad_b.reshape(256)


def solution(mesh):
    fine = Mesh(mesh.devices.reshape(SIZES), AXES)
    in_specs = (
        P((ROW + REP), None),
        P(ROW),
        P(ROW, REP, None),
        P(ROW, REP),
        P(ROW, REP, None, None, None),
        P(),
        P(),
        P((ROW + REP), None),
    )
    out_specs = (P((ROW + REP), None), P(), P())
    return jax.shard_map(shards, mesh=fine, in_specs=in_specs, out_specs=out_specs, check_vma=False)
```

```python
import functools
import math

import jax
import jax.numpy as jnp
from jax import lax
from jax.experimental import pallas as pl
from jax.experimental.pallas import tpu as pltpu
from jax.sharding import Mesh, PartitionSpec as P

AXES = ("x", "zl", "c", "zh", "y")
SIZES = (4, 4, 2, 2, 4)
ROW = ("x", "zl", "c")
REP = ("zh", "y")
FLAT = ("x", "y")
DEEP = ("zl", "zh")
F = 128
TILE = 128
SIDE = 4096
VMEM = pl.BlockSpec(memory_space=pltpu.VMEM)
SMEM = pl.BlockSpec(memory_space=pltpu.SMEM)
PARAMS = pltpu.CompilerParams(vmem_limit_bytes=40 * 1024 * 1024)


COST = pl.CostEstimate(flops=2**30, bytes_accessed=2**23, transcendentals=0)


def flat_index(x, zl, c, zh, y):
    return (((x * 4 + zl) * 2 + c) * 2 + zh) * 4 + y


def shard_moves():
    pairs = []
    for x in range(4):
        for zl in range(4):
            for c in range(2):
                for zh in range(2):
                    for y in range(4):
                        group = x * 2 + zl // 2
                        to_x = (x + 2 + group % 4 - y) % 4
                        to_zl = 2 * ((zl // 2) ^ zh ^ (group // 4)) + zl % 2
                        pairs.append(
                            (
                                flat_index(x, zl, c, zh, y),
                                flat_index(to_x, to_zl, c, group // 4, group % 4),
                            )
                        )
    return pairs


def repeat(block, count):
    return jnp.broadcast_to(block[None], (count,) + block.shape)


def exchange(block, axes):
    return lax.all_to_all(block, axes, 0, 0, tiled=True)


def scale_kernel(own_inv, features, scaled, inv):
    for half in range(2):
        wide = jnp.broadcast_to(own_inv[half : half + 1, :], (TILE, F)).T
        rows = pl.ds(half * TILE, TILE)
        inv[rows, :] = wide
        scaled[rows, :] = (features[rows, :].astype(jnp.float32) * wide).astype(jnp.bfloat16)


def stage_kernel(tiles, start, staged, token, sems):
    copies = [
        pltpu.make_async_copy(tiles.at[i], staged.at[i], sems.at[i]) for i in range(16)
    ]
    for copy in copies:
        copy.start()
    token[...] = start[...]
    for copy in copies:
        copy.wait()


def join_kernel(a, b, c, d, token, out):
    for i, part in enumerate((a, b, c, d)):
        out[i * 256 : (i + 1) * 256, :] = part[...]


def list_kernel(cols, counts, after, lists):
    core, zh, y = lax.axis_index("c"), lax.axis_index("zh"), lax.axis_index("y")
    x0 = zh * 2 + (y >> 1) + 2 + y
    z1 = (y & 1) ^ zh
    rows = lax.broadcasted_iota(jnp.int32, (24, 16), 0)
    total = jnp.zeros((24, 16), jnp.int32)
    lengths = [jnp.zeros((1, 16), jnp.int32) for _ in range(2)]
    for slab in range(4):
        side = (core ^ slab) & 1
        for k in range(4):
            col = cols[slab, k : k + 1, :]
            at_x = (lax.axis_index("x") - x0 + (col >> 1)) & 3
            at_z = (((z1 ^ (col >> 3)) << 1) + slab // 2) ^ lax.axis_index("zl")
            code = ((at_x * 4 + at_z) * 2 + (col & 1)) * TILE + (slab * 4 + k) * SIDE
            live = counts[slab : slab + 1, :] > k
            length = jnp.where(side == 0, lengths[0], lengths[1] + 8)
            total += jnp.where((rows == length) & live, code, 0)
            lengths = [
                lengths[i] + jnp.where(live & (side == i), 1, 0) for i in range(2)
            ]
    total = jnp.where(rows == 16, lengths[0], total)
    lists[...] = jnp.where(rows == 17, lengths[1], total)


def half_products(side, lists, tiles, feats, use, count, blocks_of):
    def one(block, pairs):
        length = lists[16 + side, block]
        total = jnp.zeros((TILE, F), jnp.float32)
        for pair in range(pairs):
            picks, chosen = [], []
            for slot in (2 * pair, 2 * pair + 1):
                at = slot if slot < 2 else jnp.minimum(slot, length - 1)
                code = lists[8 * side + at, block]
                begin = pl.multiple_of(code & (SIDE - 1), TILE)
                pick = feats[pl.ds(begin, TILE), :]
                if slot >= 2:
                    pick = jnp.where(slot < length, pick, jnp.zeros_like(pick))
                picks.append(pick)
                chosen.append(tiles[block, code >> 12])
            total += jnp.dot(
                jnp.concatenate(chosen, axis=1),
                jnp.concatenate(picks, axis=0),
                preferred_element_type=jnp.float32,
            )
        use(block, total)

    def some(blocks):
        length = functools.reduce(jnp.maximum, [lists[16 + side, block] for block in blocks])
        for pairs in range(1, 5):

            @pl.when((length + 1) >> 1 == pairs)
            def _(pairs=pairs):
                for block in blocks:
                    one(block, pairs)

    lax.fori_loop(0, count, lambda step, _: some(blocks_of(step)), None)


def join(parts, feats):
    for i, part in enumerate(parts):
        feats[i * 1024 : (i + 1) * 1024, :] = part[...]


def own_kernel(lists, tiles, a, b, c, d, out, feats):
    join((a, b, c, d), feats)

    def use(block, total):
        out[block] = total

    half_products(0, lists, tiles, feats, use, 4, lambda step: [step * 4 + i for i in range(4)])


def other_kernel(shifts, lists, tiles, a, b, c, d, begun, *refs):
    feats = refs[-1]
    join((a, b, c, d), feats)
    for shift, out in zip(shifts, refs[-1 - len(shifts) : -1]):
        share = (lax.axis_index("y") + shift) & 3

        def use(block, total, out=out):
            out[block >> 3, block & 1] = (total + begun[block]).astype(out.dtype)

        half_products(
            1, lists, tiles, feats, use, 1, lambda step: [share * 2 + i for i in (0, 1, 8, 9)]
        )


def add_up(parts, count):
    terms = [parts[i] for i in range(count)]
    while len(terms) > 1:
        terms = [a + b for a, b in zip(terms[::2], terms[1::2])]
    return terms[0]


def far_sum_kernel(a, b, c, d, out):
    far = 1 - lax.axis_index("zh")
    out[...] = add_up([r[far].astype(jnp.float32) for r in (a, b, c, d)], 4).astype(out.dtype)


def dense_kernel(a, b, c, d, far, inv, weight, bias, cotangent, hidden, grads):
    near = lax.axis_index("zh")
    summed = add_up([r[near].astype(jnp.float32) for r in (a, b, c, d)], 4)
    summed += far[...].astype(jnp.float32)
    aggregated = (summed * inv[...]).astype(jnp.bfloat16)
    pre_act = jnp.dot(aggregated, weight[...], preferred_element_type=jnp.float32) + bias[...]
    sig = 1.0 / (1.0 + jnp.exp(-pre_act))
    hidden[...] = (pre_act * sig).astype(jnp.bfloat16)
    pre_grad = (
        cotangent[...].astype(jnp.float32) * sig * (1.0 + pre_act * (1.0 - sig))
    ).astype(jnp.bfloat16)
    grad_w = lax.dot_general(
        aggregated, pre_grad, (((0,), (0,)), ((), ())), preferred_element_type=jnp.float32
    )
    grad_b = jnp.sum(pre_grad.astype(jnp.float32), axis=0, keepdims=True)
    grad_b = jnp.concatenate([grad_b[:, :128], grad_b[:, 128:]] * 4, axis=0)
    for i in range(16):
        grads[i] = jnp.concatenate([grad_w[i * 8 : i * 8 + 8], grad_b], axis=1)


def first_sum_kernel(parts, out):
    out[...] = add_up(parts, 16)


def pair_sum_kernel(mine, theirs, out):
    total = mine[...] + theirs[...]
    for i in range(8):
        out[i] = total


def last_sum_kernel(scale, parts, grad_w, grad_b):
    total = add_up(parts, 8) * scale
    for i in range(16):
        grad_w[i] = total[:, 0:256]
    grad_b[...] = jnp.concatenate([total[0:1, 256:384], total[1:2, 256:384]], axis=1)


def shards(features, degrees, tile_cols, tile_counts, tiles, weight, bias, cotangent):
    span_rows = features.shape[0]
    core = lax.axis_index("c")
    zh = lax.axis_index("zh")
    y = lax.axis_index("y")
    rep_index = zh * 4 + y
    own_degrees = lax.dynamic_slice_in_dim(degrees, (zh * 4 + y) * span_rows, span_rows)
    own_inv = lax.rsqrt(own_degrees.astype(jnp.float32)).reshape(2, TILE)
    scaled, inv_wide = pl.pallas_call(
        scale_kernel,
        out_shape=(
            jax.ShapeDtypeStruct((span_rows, F), jnp.bfloat16),
            jax.ShapeDtypeStruct((span_rows, F), jnp.float32),
        ),
        grid=(1,),
        in_specs=[
            pl.BlockSpec((2, TILE), lambda i: (0, 0)),
            pl.BlockSpec((span_rows, F), lambda i: (0, 0)),
        ],
        out_specs=(VMEM, VMEM),
        compiler_params=PARAMS,
        name="scale",
    )(own_inv, features)

    moved = lax.ppermute(scaled, AXES, shard_moves())
    staged, token = pl.pallas_call(
        stage_kernel,
        out_shape=(
            jax.ShapeDtypeStruct((16, 16, TILE, TILE), tiles.dtype),
            jax.ShapeDtypeStruct((8, F), jnp.float32),
        ),
        grid=(1,),
        in_specs=[
            pl.BlockSpec(memory_space=pl.ANY),
            pl.BlockSpec((8, F), lambda i: (0, 0)),
        ],
        out_specs=(VMEM, VMEM),
        scratch_shapes=[pltpu.SemaphoreType.DMA((16,))],
        compiler_params=PARAMS,
        cost_estimate=pl.CostEstimate(flops=0, bytes_accessed=16 * 2**20, transcendentals=0),
        name="stage",
    )(tiles.reshape(16, 16, TILE, TILE), inv_wide)
    along_z = pl.pallas_call(
        join_kernel,
        out_shape=jax.ShapeDtypeStruct((4 * span_rows, F), jnp.bfloat16),
        in_specs=[VMEM] * 5,
        out_specs=VMEM,
        compiler_params=PARAMS,
        name="join",
    )(
        moved,
        *(lax.ppermute(moved, "zl", [(i, i ^ flip) for i in range(4)]) for flip in (1, 2, 3)),
        token,
    )
    own = {0: along_z}
    for shift in (1, 3, 2):
        own[shift] = lax.ppermute(along_z, "x", [(i, (i + shift) % 4) for i in range(4)])
    other = {shift: lax.ppermute(own[shift], "c", [(0, 1), (1, 0)]) for shift in (0, 1, 3, 2)}
    own, other = ([pieces[shift] for shift in range(4)] for pieces in (own, other))
    lists = pl.pallas_call(
        list_kernel,
        out_shape=jax.ShapeDtypeStruct((24, 16), jnp.int32),
        grid=(1,),
        in_specs=[
            pl.BlockSpec((4, 4, 16), lambda i: (0, 0, 0)),
            pl.BlockSpec((4, 16), lambda i: (0, 0)),
            pl.BlockSpec(memory_space=pl.ANY),
        ],
        out_specs=pl.BlockSpec((24, 16), lambda i: (0, 0)),
        compiler_params=PARAMS,
        name="list",
    )(tile_cols.transpose(1, 2, 0), tile_counts.T, own[3])
    begun = pl.pallas_call(
        own_kernel,
        in_specs=[SMEM] + [VMEM] * 5,
        out_specs=VMEM,
        out_shape=jax.ShapeDtypeStruct((16, TILE, F), jnp.float32),
        scratch_shapes=[pltpu.VMEM((SIDE, F), jnp.bfloat16)],
        compiler_params=PARAMS,
        cost_estimate=COST,
        name="own_half",
    )(lists, staged, *own)
    def other_half(shifts, after):
        parts = pl.pallas_call(
            functools.partial(other_kernel, shifts),
            in_specs=[SMEM] + [VMEM] * 6 + [pl.BlockSpec(memory_space=pl.ANY)] * len(after),
            out_specs=[VMEM] * len(shifts),
            scratch_shapes=[pltpu.VMEM((SIDE, F), jnp.bfloat16)],
            out_shape=[jax.ShapeDtypeStruct((2, 2, TILE, F), jnp.bfloat16)] * len(shifts),
            compiler_params=PARAMS,
            cost_estimate=COST,
            name="other_half",
        )(lists, staged, *other, begun, *after)
        return [part.reshape(2, span_rows, F) for part in parts]

    sent = other_half((2, 1, 3), ())
    parts = [
        lax.ppermute(part, "y", [(i, (i + shift) % 4) for i in range(4)])
        for part, shift in zip(sent, (2, 1, 3))
    ] + other_half((0,), sent[:1])
    far = pl.pallas_call(
        far_sum_kernel,
        out_shape=jax.ShapeDtypeStruct((span_rows, F), jnp.bfloat16),
        in_specs=[VMEM] * 4,
        out_specs=VMEM,
        compiler_params=PARAMS,
        name="far_sum",
    )(*parts)
    far = lax.ppermute(far, "zh", [(0, 1), (1, 0)])
    hidden, grads = pl.pallas_call(
        dense_kernel,
        out_shape=(
            jax.ShapeDtypeStruct((span_rows, 256), jnp.bfloat16),
            jax.ShapeDtypeStruct((16, 8, 384), jnp.float32),
        ),
        in_specs=[VMEM] * 9,
        out_specs=(VMEM, VMEM),
        compiler_params=PARAMS,
        name="dense",
    )(*parts, far, inv_wide, weight, bias.reshape(1, 256), cotangent)

    grads = exchange(grads, FLAT)
    grads = pl.pallas_call(
        first_sum_kernel,
        out_shape=jax.ShapeDtypeStruct((8, 384), jnp.float32),
        in_specs=[VMEM],
        out_specs=VMEM,
        compiler_params=PARAMS,
        name="first_sum",
    )(grads)
    grads = pl.pallas_call(
        pair_sum_kernel,
        out_shape=jax.ShapeDtypeStruct((8, 8, 384), jnp.float32),
        in_specs=[VMEM, VMEM],
        out_specs=VMEM,
        compiler_params=PARAMS,
        name="pair_sum",
    )(grads, lax.ppermute(grads, "c", [(0, 1), (1, 0)]))
    grads = exchange(grads, DEEP)
    grad_w, grad_b = pl.pallas_call(
        functools.partial(last_sum_kernel, 1.0 / math.sqrt(span_rows * math.prod(SIZES))),
        out_shape=(
            jax.ShapeDtypeStruct((16, 8, 256), jnp.float32),
            jax.ShapeDtypeStruct((1, 256), jnp.float32),
        ),
        in_specs=[VMEM],
        out_specs=(VMEM, VMEM),
        compiler_params=PARAMS,
        name="last_sum",
    )(grads)
    grad_w = exchange(grad_w, FLAT).reshape(128, 256)
    return hidden, grad_w, grad_b.reshape(256)


def solution(mesh):
    fine = Mesh(mesh.devices.reshape(SIZES), AXES)
    in_specs = (
        P((ROW + REP), None),
        P(ROW),
        P(ROW, REP, None),
        P(ROW, REP),
        P(ROW, REP, None, None, None),
        P(),
        P(),
        P((ROW + REP), None),
    )
    out_specs = (P((ROW + REP), None), P(), P())
    return jax.shard_map(shards, mesh=fine, in_specs=in_specs, out_specs=out_specs, check_vma=False)
```
